32 devices in a mesh: rep: 2 (over x), node: 2 (over core), local: 8 (over z, y).
Axes of the slice: x: 2, y: 2, z: 4, core: 2. Of those that a mesh axis runs over, the one named last changes fastest.
Arguments:
- attn_out: bfloat16 [64, 1024], P(('rep', 'node'), 'local'), parts along dimension 0, may hold values from -6 to 6
- o_proj: bfloat16 [1024, 7168], P('local'), may hold values from -0.1875 to 0.1875
- resid: bfloat16 [64, 7168], P(('rep', 'node', 'local')), parts along dimension 0, may hold values from -6 to 6
- norm_gain: float32 [7168], replicated, may hold values from 0.5 to 1.5
- routes: int32 [64, 8], P(('rep', 'node', 'local')), parts along dimension 0, may hold values from 0 to 15, all different within a row; in each aligned block of 2 rows (0 to 1, 2 to 3, ...) at most 2 rows name the same one
- route_w: bfloat16 [64, 8], P(('rep', 'node', 'local')), parts along dimension 0, may hold values from 0.19921875 to 1
- w_gate: bfloat16 [16, 7168, 2048], P(('node', 'local')), may hold values from -0.0625 to 0.0625
- w_up: bfloat16 [16, 7168, 2048], P(('node', 'local')), may hold values from -0.0625 to 0.0625
- w_down: bfloat16 [16, 2048, 7168], P(('node', 'local')), may hold values from -0.125 to 0.125
Outputs:
- layer_out: bfloat16 [64, 7168], P(('rep', 'node', 'local')), parts along dimension 0
The draws below stay inside these ranges and needn't reach their ends.
There are 2 independent parts, one for each index of `rep`. The reference program is written for one: setup_inputs(seed, part) draws one part's arguments, and reference() takes and returns one part's arrays. A program takes and returns all parts, laid end to end along the dimension named above; an argument that names none is the same for every part. Nothing has to cross between parts.
Inputs may be any that keep to these rules, and one draw needn't show every extreme that they name: `routes`: each row names 8 different experts. Within the rows of one device (aligned blocks of 2 rows) no expert is named more than 2 times, and in some block some expert is named exactly 2 times.
All inputs are finite; a program needn't handle non-finite values.
Results may differ from the reference program's by a relative error of at most 0.0075.
Values may be sent and summed in bfloat16 or wider, within the bound.
No kernel may reach another device: no remote copies, remote signals or barrier semaphores. Data moves between devices by JAX's collectives and lax.ppermute only.
A program may use at most 128 MiB of HBM per device.

```python
import math
import jax
import jax.numpy as jnp
import numpy as np
from jax import lax

D = 7168
FF = 2048
HD = 128
GROUP_EXPERTS = 8
TOPK = 8
TOK_DEV = 2
MOST = 2
SHARDS = 1
F_DEV = 2048
EXPERTS = 16
HEADS = 8
TOKENS = 32
N_NODE = 2
N_LOCAL = 8


def spiked(drawn, own_key, source, target, shards_of, factor):
    owner, partner = [(jnp.arange(drawn.shape[dim]) // (drawn.shape[dim] // shards_of)).reshape([-1 if axis == dim else 1 for axis in range(drawn.ndim)]) for dim in (source, target)]
    chosen = jax.random.permutation(own_key, shards_of)[partner]
    strong = (owner == chosen) | (owner == (partner + shards_of // 2) % shards_of)
    return jnp.where(strong, factor * drawn, drawn)


def levels(stream_key, extent, split, smallest, largest):
    factor_of = 1.0
    for dim, shards_of in split:
        steps = jax.random.uniform(jax.random.fold_in(jax.random.fold_in(stream_key, 6), dim), (shards_of,), jnp.float32, smallest / len(split), largest / len(split))
        factor_of = factor_of * jnp.repeat(jnp.exp(steps), extent[dim] // shards_of).reshape((-1,) + (1,) * (len(extent) - 1 - dim))
    return factor_of


def assign_block(own_key, own, number, rows, count, top, reach, lean):
    ranking = jax.random.permutation(own_key, count)
    packed, common = portions_of(count, rows * top, reach, lean, True), portions_of(count, rows * top, reach, lean, False)
    places = jnp.arange(count)

    def named(lengths, rotation):
        used = int((lengths > 0).sum())
        fixed = max(1, used // 4)
        moved = fixed + (places - fixed + rotation * (used - fixed)) % max(1, count - fixed)
        return jnp.zeros((count,), jnp.int32).at[ranking[jnp.where(places < fixed, places, moved)]].set(jnp.asarray(lengths, jnp.int32))

    lengths = jnp.where(number % 4 == 0, named(packed, number // 4), named(common, number - number // 4 - 1))
    mixed = jax.random.permutation(jax.random.fold_in(own, 3), count)
    donor, sink = mixed[0:count // 2 * 2:2], mixed[1:count // 2 * 2:2]
    margin = jnp.minimum(lengths[donor] - 1, reach - lengths[sink]) // 2
    margin = jnp.where((donor == ranking[0]) | (sink == ranking[0]) | (lengths[sink] == 0), 0, jnp.maximum(margin, 0))
    moved = jax.random.randint(jax.random.fold_in(own, 4), (count // 2,), 0, 1 << 20) % (margin + 1)
    lengths = lengths.at[donor].add(-moved).at[sink].add(moved)
    members = jnp.searchsorted(jnp.cumsum(lengths), jnp.arange(rows * top), side="right").astype(jnp.int32)
    table = members.reshape(top, rows).T
    table = table[jax.random.permutation(jax.random.fold_in(own, 1), rows)]
    rotation = jax.random.randint(jax.random.fold_in(own, 2), (rows, 1), 0, top)
    return jnp.take_along_axis(table, (jnp.arange(top)[None, :] + rotation) % top, axis=1)


def portions_of(amount, total, reach, slope, full):
    portions = [(1 << 20) // math.isqrt(grade ** slope) + 1 for grade in range(1, amount + 1)]
    largest = reach if full else min(reach, max(-(-total // amount), total * portions[0] // sum(portions)))
    least = 1 if total - largest >= amount - 1 else 0
    counts, rest = [largest] + [least] * (amount - 1), total - largest - least * (amount - 1)
    while rest > 0:
        movable = [i for i in range(1, amount) if counts[i] < largest] or [i for i in range(1, amount) if counts[i] < reach]
        pool, remaining = sum([portions[i] for i in movable]), rest
        for i in movable:
            more = min(reach - counts[i], max(1, remaining * portions[i] // pool), rest)
            counts[i] = counts[i] + more
            rest = rest - more
    return np.array(counts)


def normal_values(own_key, extent, spread, limit, cuts=(), held_as=jnp.bfloat16):
    drawn = spread * jax.random.normal(own_key, extent, jnp.float32)
    if cuts:
        drawn = drawn * levels(own_key, extent, cuts, -0.22, 0.18)
    return jnp.clip(drawn, -limit, limit).astype(held_as)


def noise_with(own_key, shape, scale, bound, cuts, heavy, kind=jnp.bfloat16):
    values = scale * jax.random.normal(own_key, shape, jnp.float32)
    if cuts:
        values = values * levels(own_key, shape, cuts, -0.22, 0.18)
    return jnp.clip(spiked(values, jax.random.fold_in(own_key, 3), *heavy), -bound, bound).astype(kind)


def setup_inputs(seed: int = 0, part: int = 0) -> dict:
    streams_of = jax.random.split(jax.random.key(seed), 10)
    part_keys = jax.random.split(jax.random.fold_in(streams_of[9], part), 10)
    attn_out = noise_with(part_keys[0], (TOKENS, HEADS * HD), 1.0, 6.0, ((0, 2), (1, 8)), (1, 0, 8, 2.0))
    o_proj = normal_values(streams_of[1], (HEADS * HD, D), (HEADS * HD) ** -0.5, 0.1875, ((0, 8),))
    resid = normal_values(part_keys[2], (TOKENS, D), 1.0, 6.0, ((0, 16),))
    norm_gain = jnp.clip(1.0 + 0.1 * jax.random.normal(streams_of[3], (D,), jnp.float32), 0.5, 1.5)
    routes_keys = jax.random.split(jax.random.fold_in(part_keys[4], 1), TOKENS // TOK_DEV)
    routes_turns = jax.random.permutation(jax.random.fold_in(part_keys[4], 3), TOKENS // TOK_DEV)
    routes = jax.vmap(lambda own, number: assign_block(jax.random.fold_in(part_keys[4], 2), own, number, TOK_DEV, EXPERTS, TOPK, MOST, 2))(routes_keys, routes_turns).reshape((TOKENS, TOPK))
    route_w = jnp.clip(0.19921875 + 0.80078125 * jax.random.uniform(part_keys[5], (TOKENS, TOPK), jnp.float32) ** levels(part_keys[5], (TOKENS, TOPK), ((0, 16),), -0.2, 0.2), 0.19921875, 1.0).astype(jnp.bfloat16)
    w_gate = normal_values(streams_of[6], (EXPERTS * SHARDS, D, F_DEV), D ** -0.5, 0.0625, ((0, 16),))
    w_up = normal_values(streams_of[7], (EXPERTS * SHARDS, D, F_DEV), D ** -0.5, 0.0625, ((0, 16),))
    w_down = normal_values(streams_of[8], (EXPERTS * SHARDS, F_DEV, D), FF ** -0.5, 0.125, ((0, 16),))
    return dict(attn_out=attn_out, o_proj=o_proj, resid=resid, norm_gain=norm_gain, routes=routes, route_w=route_w, w_gate=w_gate, w_up=w_up, w_down=w_down)


def reference(attn_out, o_proj, resid, norm_gain, routes, route_w, w_gate, w_up, w_down):
    projected = jnp.dot(attn_out, o_proj, preferred_element_type=jnp.float32)
    hidden = resid.astype(jnp.float32) + projected
    mean_sq = lax.optimization_barrier(jnp.mean(hidden * hidden, axis=-1, keepdims=True))
    normed = (hidden * lax.rsqrt(mean_sq + 1e-06) * norm_gain.astype(jnp.float32)).astype(jnp.bfloat16)
    flat_ids = routes.reshape(-1).astype(jnp.int32)
    flat_weights = route_w.reshape(-1).astype(jnp.float32)
    token_of = (jnp.arange(TOKENS * TOPK) // TOPK).astype(jnp.int32)
    row_cap = min(TOKENS, N_NODE * N_LOCAL * MOST)
    model_width = o_proj.shape[1]
    hidden_dev = w_gate.shape[2]
    group_count = EXPERTS // GROUP_EXPERTS

    def one_expert(groups, expert):
        picked = jnp.argsort((flat_ids != expert).astype(jnp.int32), stable=True)[:row_cap].astype(jnp.int32)
        usable = flat_ids[picked] == expert
        tokens = token_of[picked]
        chosen_rows = normed[tokens]
        first_row = (expert * SHARDS).astype(jnp.int32)
        gate_w = lax.dynamic_slice_in_dim(w_gate, first_row, SHARDS, 0)
        up_w = lax.dynamic_slice_in_dim(w_up, first_row, SHARDS, 0)
        down_w = lax.dynamic_slice_in_dim(w_down, first_row, SHARDS, 0)
        gate_joined = jnp.transpose(gate_w, (1, 0, 2)).reshape(model_width, SHARDS * hidden_dev)
        up_joined = jnp.transpose(up_w, (1, 0, 2)).reshape(model_width, SHARDS * hidden_dev)
        gate_val = jnp.dot(chosen_rows, gate_joined, preferred_element_type=jnp.float32)
        up_val = jnp.dot(chosen_rows, up_joined, preferred_element_type=jnp.float32)
        activated = (jax.nn.silu(gate_val) * up_val).astype(jnp.bfloat16).reshape(row_cap, SHARDS, hidden_dev)
        pieces = jnp.einsum('rsf,sfd->rsd', activated.astype(jnp.float32), down_w.astype(jnp.float32)).astype(jnp.bfloat16)
        expert_out = lax.optimization_barrier(jnp.sum(pieces.astype(jnp.float32), axis=1))
        coeffs = jnp.where(usable, flat_weights[picked], jnp.zeros_like(flat_weights[picked]))
        group_idx = expert // GROUP_EXPERTS
        groups = groups.at[group_idx, tokens].add(coeffs[:, None] * expert_out)
        return (groups, None)
    initial = jnp.zeros((group_count, TOKENS, model_width), jnp.float32)
    groups, _ = lax.scan(one_expert, initial, jnp.arange(EXPERTS, dtype=jnp.int32))
    rounded = groups.astype(jnp.bfloat16).astype(jnp.float32)
    summed = hidden
    for group_idx in range(group_count):
        summed = summed + rounded[group_idx]
    return summed.astype(jnp.bfloat16)
```

```python
import functools

import jax
import jax.numpy as jnp
from jax import lax
from jax.experimental import pallas as pl
from jax.experimental.pallas import tpu as pltpu
from jax.sharding import PartitionSpec as P

GROUP_EXPERTS = 8
LANES = 128
VMEM_OWN = 30 << 20
F32, BF16 = jnp.float32, jnp.bfloat16


def swap(x, axis, bit):
    return lax.ppermute(x, axis, [(i, i ^ bit) for i in range(lax.axis_size(axis))])


def fetch_kernel(first, rows, w_ref, after_ref, *refs):
    out_ref, sem = refs[-2:]
    part = pl.ds(first, rows)
    copy = pltpu.make_async_copy(w_ref.at[0, part], out_ref.at[part], sem)
    copy.start()
    copy.wait()


def fetch(weight, held, first, rows, after):
    _, depth, width = weight.shape
    anywhere = pl.BlockSpec(memory_space=pl.ANY)
    kept = [] if held is None else [pltpu.with_memory_space_constraint(held, pltpu.VMEM)]
    return pl.pallas_call(
        functools.partial(fetch_kernel, first, rows),
        out_shape=pltpu.VMEM((depth, width), BF16),
        in_specs=[anywhere, anywhere] + [pl.BlockSpec(memory_space=pltpu.VMEM)] * len(kept),
        out_specs=pl.BlockSpec(memory_space=pltpu.VMEM),
        scratch_shapes=[pltpu.SemaphoreType.DMA],
        input_output_aliases={2: 0} if kept else {},
        compiler_params=pltpu.CompilerParams(vmem_limit_bytes=VMEM_OWN),
        cost_estimate=pl.CostEstimate(flops=0, bytes_accessed=2 * rows * width, transcendentals=0),
    )(weight, after, *kept)


def expert_kernel(
    chunk_u, chunk_d, x_ref, mine_ref, gate_ref, up_hbm, down_hbm, keep_ref, send_ref,
    ring_u, ring_d, acc_g, acc_u, act_ref, sem_u, sem_d,
):
    rows = acc_g.shape[0]
    depth, width = gate_ref.shape
    slots_u, slots_d = ring_u.shape[0], ring_d.shape[0]
    steps_u, steps_d = depth // chunk_u, depth // chunk_d

    def copy_u(step):
        slot = step % slots_u
        return pltpu.make_async_copy(
            up_hbm.at[0, pl.ds(step * chunk_u, chunk_u)], ring_u.at[slot], sem_u.at[slot]
        )

    def copy_d(step):
        slot = step % slots_d
        return pltpu.make_async_copy(
            down_hbm.at[0, :, pl.ds(step * chunk_d, chunk_d)], ring_d.at[slot], sem_d.at[slot]
        )

    for step in range(min(slots_u, steps_u)):
        copy_u(step).start()
    for step in range(min(slots_d, steps_d)):
        copy_d(step).start()

    acc_g[...] = jnp.zeros_like(acc_g)
    acc_u[...] = jnp.zeros_like(acc_u)
    for step in range(steps_u):
        part = pl.ds(step * chunk_u, chunk_u)
        acc_g[...] += jnp.dot(x_ref[:, part], gate_ref[part, :], preferred_element_type=F32)
    for step in range(steps_u):
        part = pl.ds(step * chunk_u, chunk_u)
        copy_u(step).wait()
        acc_u[...] += jnp.dot(x_ref[:, part], ring_u[step % slots_u], preferred_element_type=F32)
        if step + slots_u < steps_u:
            copy_u(step + slots_u).start()
    gate_val = acc_g[...]
    act_ref[...] = (gate_val / (1.0 + jnp.exp(-gate_val)) * acc_u[...]).astype(BF16)
    coeff = jnp.sum(x_ref[:, pl.ds(depth, LANES)].astype(F32) * mine_ref[...], axis=1, keepdims=True)
    half = rows // 2
    for step in range(steps_d):
        part = pl.ds(step * chunk_d, chunk_d)
        copy_d(step).wait()
        piece = jnp.dot(act_ref[...], ring_d[step % slots_d], preferred_element_type=F32) * coeff
        keep_ref[:, part] = piece[:half]
        send_ref[:, part] = piece[half:].astype(BF16)
        if step + slots_d < steps_d:
            copy_d(step + slots_d).start()


def expert(x, mine, gate, w_up, w_down):
    rows = x.shape[0]
    depth, width = gate.shape
    chunk_u, chunk_d = depth // 7, depth // 7
    slots_u, slots_d = 3, 3
    vmem = pl.BlockSpec(memory_space=pltpu.VMEM)
    anywhere = pl.BlockSpec(memory_space=pl.ANY)
    return pl.pallas_call(
        functools.partial(expert_kernel, chunk_u, chunk_d),
        out_shape=(
            jax.ShapeDtypeStruct((rows // 2, depth), F32),
            jax.ShapeDtypeStruct((rows // 2, depth), BF16),
        ),
        in_specs=[vmem, vmem, vmem, anywhere, anywhere],
        out_specs=(vmem, vmem),
        scratch_shapes=[
            pltpu.VMEM((slots_u, chunk_u, width), BF16),
            pltpu.VMEM((slots_d, width, chunk_d), BF16),
            pltpu.VMEM((rows, width), F32),
            pltpu.VMEM((rows, width), F32),
            pltpu.VMEM((rows, width), BF16),
            pltpu.SemaphoreType.DMA((slots_u,)),
            pltpu.SemaphoreType.DMA((slots_d,)),
        ],
        compiler_params=pltpu.CompilerParams(vmem_limit_bytes=VMEM_OWN),
        cost_estimate=pl.CostEstimate(
            flops=6 * rows * depth * width, bytes_accessed=4 * depth * width, transcendentals=rows * width
        ),
    )(x, mine, pltpu.with_memory_space_constraint(gate, pltpu.VMEM), w_up, w_down)


def shards(attn_out, o_proj, resid, norm_gain, routes, route_w, w_gate, w_up, w_down):
    tok_rows, depth = resid.shape
    n_local, n_node = lax.axis_size("local"), lax.axis_size("node")
    expert_count = n_node * GROUP_EXPERTS
    shard_count = n_local // GROUP_EXPERTS
    here = lax.axis_index("local")
    mine = (lax.axis_index("node") * n_local + here) // shard_count
    bits = [1 << b for b in range(n_local.bit_length() - 1)]

    flip = [sum(bit for b, bit in enumerate(reversed(bits)) if j >> b & 1) for j in range(n_local)]
    owner = jnp.repeat(here ^ jnp.array(flip, jnp.int32), tok_rows) * tok_rows
    owner = owner + jnp.tile(jnp.arange(tok_rows, dtype=jnp.int32), n_local)
    order = (owner[:, None] == jnp.arange(n_local * tok_rows, dtype=jnp.int32)[None, :]).astype(BF16)

    hot = routes[:, :, None] == jnp.arange(LANES, dtype=jnp.int32)[None, None, :]
    picks = jnp.sum(jnp.where(hot, route_w.astype(F32)[:, :, None], 0.0), axis=1)
    mine_hot = (jnp.arange(LANES, dtype=jnp.int32) == mine).astype(F32)[None, :]
    order, picks, mine_hot = lax.optimization_barrier((order, picks, mine_hot))
    ordered = jnp.dot(order, attn_out, preferred_element_type=F32).astype(BF16)

    steps = len(bits) * 2
    unit = depth // 28
    cuts = [unit * (28 * s // steps) for s in range(steps + 1)]
    held = None

    def send(x, axis, bit, step):
        nonlocal held
        got = swap(x, axis, bit)
        held = fetch(w_gate, held, cuts[step], cuts[step + 1] - cuts[step], x)
        got, held = lax.optimization_barrier((got, held))
        return got

    w_gate, w_up, w_down = [pltpu.with_memory_space_constraint(w, pltpu.HBM) for w in (w_gate, w_up, w_down)]
    step = 0
    partial = jnp.dot(ordered, o_proj, preferred_element_type=F32)
    for bit in bits[:-1]:
        half = partial.shape[0] // 2
        partial = partial[:half] + send(partial[half:].astype(BF16), "local", bit, step).astype(F32)
        step += 1
    partial = jnp.concatenate([partial[:tok_rows] + resid.astype(F32), partial[tok_rows:]], axis=0)
    out = jnp.concatenate(
        [partial, jnp.concatenate([picks, jnp.zeros((tok_rows, LANES), F32)], axis=0)], axis=1
    ).astype(BF16)
    got = send(out, "local", bits[-1], step).astype(F32)
    step += 1
    got = jnp.concatenate([got[tok_rows:], got[:tok_rows]], axis=0)
    hidden = partial + got[:, :depth]
    columns = jnp.concatenate([picks, got[tok_rows:, depth:]], axis=0)
    mean_sq = jnp.mean(hidden * hidden, axis=-1, keepdims=True)
    normed = hidden * lax.rsqrt(mean_sq + 1e-06) * norm_gain
    tokens = jnp.concatenate([normed, columns], axis=1).astype(BF16)
    for bit in reversed(bits[:-1]):
        tokens = jnp.concatenate([tokens, send(tokens, "local", bit, step)], axis=0)
        step += 1
    tokens = jnp.concatenate([tokens, send(tokens, "node", 1, step)], axis=0)

    keep, away = expert(tokens, mine_hot, held, w_up, w_down)
    keep = keep + swap(away, "node", 1).astype(F32)
    for bit in bits:
        half = keep.shape[0] // 2
        keep = keep[:half] + swap(keep[half:].astype(BF16), "local", bit).astype(F32)
    return (hidden[:tok_rows] + keep).astype(BF16)


def solution(mesh):
    placed = (
        P(("rep", "node"), "local"),
        P("local", None),
        P(("rep", "node", "local"), None),
        P(),
        P(("rep", "node", "local"), None),
        P(("rep", "node", "local"), None),
        P(("node", "local"), None, None),
        P(("node", "local"), None, None),
        P(("node", "local"), None, None),
    )
    return jax.shard_map(
        shards,
        mesh=mesh,
        in_specs=placed,
        out_specs=P(("rep", "node", "local"), None),
        check_vma=False,
    )
```

```python
import functools

import jax
import jax.numpy as jnp
from jax import lax
from jax.experimental import pallas as pl
from jax.experimental.pallas import tpu as pltpu
from jax.sharding import PartitionSpec as P

GROUP_EXPERTS = 8
LANES = 128
VMEM_OWN = 26 << 20
SLOTS = 4
HAVE = 1
F32, BF16 = jnp.float32, jnp.bfloat16
VMEM = pl.BlockSpec(memory_space=pltpu.VMEM)
ANYWHERE = pl.BlockSpec(memory_space=pl.ANY)


def swap(x, axis, bit):
    return lax.ppermute(x, axis, [(i, i ^ bit) for i in range(lax.axis_size(axis))])


def in_vmem(x):
    return pltpu.with_memory_space_constraint(x, pltpu.VMEM)


def project_kernel(n_local, tok_rows, attn_ref, proj_ref, keep_ref, send_ref):
    count = n_local * tok_rows
    here = lax.axis_index("local")
    place = lax.broadcasted_iota(jnp.int32, (count, count), 0)
    block, flip = place // tok_rows, 0
    bits = n_local.bit_length() - 1
    for b in range(bits):
        flip = flip | (((block >> b) & 1) << (bits - 1 - b))
    owner = (here ^ flip) * tok_rows + place % tok_rows
    order = (owner == lax.broadcasted_iota(jnp.int32, (count, count), 1)).astype(BF16)
    ordered = jnp.dot(order, attn_ref[...], preferred_element_type=F32).astype(BF16)
    half = count // 2
    partial = jnp.dot(ordered, proj_ref[...], preferred_element_type=F32)
    keep_ref[...] = partial[:half]
    send_ref[...] = partial[half:].astype(BF16)


def project(attn_out, o_proj, tok_rows):
    depth = o_proj.shape[1]
    half = attn_out.shape[0] // 2
    return pl.pallas_call(
        functools.partial(project_kernel, lax.axis_size("local"), tok_rows),
        out_shape=(pltpu.VMEM((half, depth), F32), pltpu.VMEM((half, depth), BF16)),
        in_specs=[VMEM, VMEM],
        out_specs=(VMEM, VMEM),
        compiler_params=pltpu.CompilerParams(vmem_limit_bytes=VMEM_OWN),
    )(attn_out, o_proj)


def fetch_kernel(depth, first, last, gate_hbm, up_hbm, after_ref, *refs):
    held_ref, sem = refs[-2:]
    copies = []
    if first < depth:
        part = pl.ds(first, min(last, depth) - first)
        copies.append(pltpu.make_async_copy(gate_hbm.at[0, part], held_ref.at[part], sem.at[0]))
    if last > depth:
        first = max(first, depth)
        source = up_hbm.at[0, pl.ds(first - depth, last - first)]
        copies.append(pltpu.make_async_copy(source, held_ref.at[pl.ds(first, last - first)], sem.at[1]))
    for copy in copies:
        copy.start()
    for copy in copies:
        copy.wait()


def fetch(w_gate, w_up, held, total, first, last, after):
    _, depth, width = w_gate.shape
    kept = [] if held is None else [in_vmem(held)]
    return pl.pallas_call(
        functools.partial(fetch_kernel, depth, first, last),
        out_shape=pltpu.VMEM((total, width), BF16),
        in_specs=[ANYWHERE] * 3 + [VMEM] * len(kept),
        out_specs=VMEM,
        scratch_shapes=[pltpu.SemaphoreType.DMA((2,))],
        input_output_aliases={3: 0} if kept else {},
        compiler_params=pltpu.CompilerParams(vmem_limit_bytes=VMEM_OWN),
        cost_estimate=pl.CostEstimate(flops=0, bytes_accessed=2 * (last - first) * width, transcendentals=0),
    )(w_gate, w_up, after, *kept)


def picks_kernel(routes_ref, route_w_ref, after_ref, picks_ref):
    tok_rows, top = routes_ref.shape
    lane = lax.broadcasted_iota(jnp.int32, (tok_rows, LANES), 1)
    total = jnp.zeros((tok_rows, LANES), F32)
    weights = route_w_ref[...].astype(F32)
    for k in range(top):
        total = total + jnp.where(routes_ref[:, k : k + 1] == lane, weights[:, k : k + 1], 0.0)
    picks_ref[...] = total


def picks_of(routes, route_w, after):
    return pl.pallas_call(
        picks_kernel,
        out_shape=pltpu.VMEM((routes.shape[0], LANES), F32),
        in_specs=[VMEM, VMEM, ANYWHERE],
        out_specs=VMEM,
        compiler_params=pltpu.CompilerParams(vmem_limit_bytes=VMEM_OWN),
    )(routes, route_w, after)


def expert_kernel(
    n_local, chunk, own_ref, other_ref, held_ref, up_hbm, down_hbm, keep_ref, send_ref,
    ring, x_ref, acc_g, acc_u, act_ref, sem,
):
    half = own_ref.shape[0]
    _, depth, width = up_hbm.shape
    slots, parts = ring.shape[0], width // chunk
    have = held_ref.shape[0] - depth
    steps = [(True, at) for at in range(have, depth, chunk)] + [(False, at) for at in range(0, depth, chunk)]

    def copies(step):
        is_up, at = steps[step]
        slot = step % slots
        for p in range(parts):
            cut = pl.ds(p * chunk, chunk)
            source = up_hbm.at[0, pl.ds(at, chunk), cut] if is_up else down_hbm.at[0, cut, pl.ds(at, chunk)]
            yield pltpu.make_async_copy(source, ring.at[slot, cut], sem.at[slot, p])

    def start(step):
        for copy in copies(step):
            copy.start()

    for step in range(min(slots, len(steps))):
        start(step)
    x_ref[:half] = own_ref[:, :depth]
    x_ref[half:] = other_ref[:, :depth]
    shard_count = n_local // GROUP_EXPERTS
    mine = (lax.axis_index("node") * n_local + lax.axis_index("local")) // shard_count
    mine_hot = lax.broadcasted_iota(jnp.int32, (1, LANES), 1) == mine
    coeff = jnp.concatenate(
        [
            jnp.sum(jnp.where(mine_hot, ref[:, depth:].astype(F32), 0.0), axis=1, keepdims=True)
            for ref in (own_ref, other_ref)
        ],
        axis=0,
    )

    def add(acc, w_ref, row, column):
        rows, columns = w_ref.shape
        part = pl.ds(column, columns)
        product = jnp.dot(x_ref[:, row : row + rows], w_ref[...], preferred_element_type=F32)
        acc[:, part] = product if row == 0 else acc[:, part] + product

    for row in range(0, depth, chunk):
        add(acc_g, held_ref.at[pl.ds(row, chunk)], row, 0)
    for row in range(0, have, chunk):
        add(acc_u, held_ref.at[pl.ds(depth + row, chunk)], row, 0)
    for step, (is_up, at) in enumerate(steps):
        slot = step % slots
        for copy in copies(step):
            copy.wait()
        if is_up:
            for p in range(parts):
                add(acc_u, ring.at[slot, pl.ds(p * chunk, chunk)], at, p * chunk)
        else:
            if at == 0:
                gate_val = acc_g[...]
                act_ref[...] = (gate_val / (1.0 + jnp.exp(-gate_val)) * acc_u[...]).astype(BF16)
            piece = jnp.dot(act_ref[...], ring[slot], preferred_element_type=F32) * coeff
            keep_ref[:, pl.ds(at, chunk)] = piece[:half]
            send_ref[:, pl.ds(at, chunk)] = piece[half:].astype(BF16)
        if step + slots < len(steps):
            start(step + slots)


def expert(own, other, held, w_up, w_down, chunk):
    half = own.shape[0]
    rows = 2 * half
    _, depth, width = w_up.shape
    slots = SLOTS
    return pl.pallas_call(
        functools.partial(expert_kernel, lax.axis_size("local"), chunk),
        out_shape=(jax.ShapeDtypeStruct((half, depth), F32), jax.ShapeDtypeStruct((half, depth), BF16)),
        in_specs=[VMEM, VMEM, VMEM, ANYWHERE, ANYWHERE],
        out_specs=(VMEM, VMEM),
        scratch_shapes=[
            pltpu.VMEM((slots, width, chunk), BF16),
            pltpu.VMEM((rows, depth), BF16),
            pltpu.VMEM((rows, width), F32),
            pltpu.VMEM((rows, width), F32),
            pltpu.VMEM((rows, width), BF16),
            pltpu.SemaphoreType.DMA((slots, width // chunk)),
        ],
        compiler_params=pltpu.CompilerParams(vmem_limit_bytes=VMEM_OWN),
        cost_estimate=pl.CostEstimate(
            flops=6 * rows * depth * width, bytes_accessed=4 * depth * width, transcendentals=rows * width
        ),
    )(own, other, in_vmem(held), w_up, w_down)


def shards(attn_out, o_proj, resid, norm_gain, routes, route_w, w_gate, w_up, w_down):
    tok_rows, depth = resid.shape
    width = w_gate.shape[2]
    n_local = lax.axis_size("local")
    bits = [1 << b for b in range(n_local.bit_length() - 1)]
    w_gate, w_up, w_down = [pltpu.with_memory_space_constraint(w, pltpu.HBM) for w in (w_gate, w_up, w_down)]

    chunk = min(1024, width)
    total = depth + HAVE * chunk
    shares = [1] + [3] + [2] * (2 * len(bits) - 3) + [3, 1]
    unit = depth // 28
    cuts = [total // unit * sum(shares[:s]) // sum(shares) * unit for s in range(len(shares) + 1)]
    held, step = fetch(w_gate, w_up, None, total, 0, cuts[1], attn_out), 1
    attn_out, held = lax.optimization_barrier((attn_out, held))

    def send(x, axis, bit, more=()):
        nonlocal held, step
        got = swap(x, axis, bit)
        held = fetch(w_gate, w_up, held, total, cuts[step], cuts[step + 1], x)
        got, held, *more = lax.optimization_barrier((got, held, *more))
        step += 1
        return (got, *more) if more else got

    keep, away = project(attn_out, o_proj, tok_rows)
    got, picks = send(away, "local", bits[0], (picks_of(routes, route_w, away),))
    partial = keep + got.astype(F32)
    for bit in bits[1:-1]:
        half = partial.shape[0] // 2
        partial = partial[:half] + send(partial[half:].astype(BF16), "local", bit).astype(F32)
    partial = jnp.concatenate([partial[:tok_rows] + resid.astype(F32), partial[tok_rows:]], axis=0)
    out = jnp.concatenate(
        [partial, jnp.concatenate([picks, jnp.zeros((tok_rows, LANES), F32)], axis=0)], axis=1
    ).astype(BF16)
    got = send(out, "local", bits[-1]).astype(F32)
    got = jnp.concatenate([got[tok_rows:], got[:tok_rows]], axis=0)
    hidden = partial + got[:, :depth]
    columns = jnp.concatenate([picks, got[tok_rows:, depth:]], axis=0)
    mean_sq = jnp.mean(hidden * hidden, axis=-1, keepdims=True)
    normed = hidden * lax.rsqrt(mean_sq + 1e-06) * norm_gain
    tokens = jnp.concatenate([normed, columns], axis=1).astype(BF16)
    for bit in reversed(bits[:-1]):
        tokens = jnp.concatenate([tokens, send(tokens, "local", bit)], axis=0)
    other = send(tokens, "node", 1)

    keep, away = expert(tokens, other, held, w_up, w_down, chunk)
    keep = keep + swap(away, "node", 1).astype(F32)
    for bit in bits:
        half = keep.shape[0] // 2
        keep = keep[:half] + swap(keep[half:].astype(BF16), "local", bit).astype(F32)
    return (hidden[:tok_rows] + keep).astype(BF16)


def solution(mesh):
    placed = (
        P(("rep", "node"), "local"),
        P("local", None),
        P(("rep", "node", "local"), None),
        P(),
        P(("rep", "node", "local"), None),
        P(("rep", "node", "local"), None),
        P(("node", "local"), None, None),
        P(("node", "local"), None, None),
        P(("node", "local"), None, None),
    )
    return jax.shard_map(
        shards,
        mesh=mesh,
        in_specs=placed,
        out_specs=P(("rep", "node", "local"), None),
        check_vma=False,
    )
```

```python
import functools

import jax
import jax.numpy as jnp
from jax import lax
from jax.experimental import pallas as pl
from jax.experimental.pallas import tpu as pltpu
from jax.sharding import PartitionSpec as P

GROUP_EXPERTS = 8
LANES = 128
VMEM_OWN = 26 << 20
SLOTS = 4
HAVE = 1
F32, BF16 = jnp.float32, jnp.bfloat16
VMEM = pl.BlockSpec(memory_space=pltpu.VMEM)
ANYWHERE = pl.BlockSpec(memory_space=pl.ANY)


def swap(x, axis, bit):
    return lax.ppermute(x, axis, [(i, i ^ bit) for i in range(lax.axis_size(axis))])


def in_vmem(x):
    return pltpu.with_memory_space_constraint(x, pltpu.VMEM)


def project_kernel(n_local, attn_ref, proj_ref, routes_ref, route_w_ref, keep_ref, send_ref, picks_ref):
    tok_rows, top = routes_ref.shape
    count = n_local * tok_rows
    here = lax.axis_index("local")
    place = lax.broadcasted_iota(jnp.int32, (count, count), 0)
    block, flip = place // tok_rows, 0
    bits = n_local.bit_length() - 1
    for b in range(bits):
        flip = flip | (((block >> b) & 1) << (bits - 1 - b))
    owner = (here ^ flip) * tok_rows + place % tok_rows
    order = (owner == lax.broadcasted_iota(jnp.int32, (count, count), 1)).astype(BF16)
    ordered = jnp.dot(order, attn_ref[...], preferred_element_type=F32).astype(BF16)
    half = count // 2
    partial = jnp.dot(ordered, proj_ref[...], preferred_element_type=F32)
    keep_ref[...] = partial[:half]
    send_ref[...] = partial[half:].astype(BF16)
    lane = lax.broadcasted_iota(jnp.int32, (tok_rows, LANES), 1)
    total = jnp.zeros((tok_rows, LANES), F32)
    weights = route_w_ref[...].astype(F32)
    for k in range(top):
        total = total + jnp.where(routes_ref[:, k : k + 1] == lane, weights[:, k : k + 1], 0.0)
    picks_ref[...] = total


def project(attn_out, o_proj, routes, route_w):
    depth = o_proj.shape[1]
    half = attn_out.shape[0] // 2
    return pl.pallas_call(
        functools.partial(project_kernel, lax.axis_size("local")),
        out_shape=(
            pltpu.VMEM((half, depth), F32),
            pltpu.VMEM((half, depth), BF16),
            pltpu.VMEM((routes.shape[0], LANES), F32),
        ),
        in_specs=[VMEM] * 4,
        out_specs=(VMEM, VMEM, VMEM),
        compiler_params=pltpu.CompilerParams(vmem_limit_bytes=VMEM_OWN),
    )(attn_out, o_proj, routes, route_w)


def fetch_kernel(depth, first, last, gate_hbm, up_hbm, after_ref, *refs):
    held_ref, sem = refs[-2:]
    copies = []
    if first < depth:
        part = pl.ds(first, min(last, depth) - first)
        copies.append(pltpu.make_async_copy(gate_hbm.at[0, part], held_ref.at[part], sem.at[0]))
    if last > depth:
        first = max(first, depth)
        source = up_hbm.at[0, pl.ds(first - depth, last - first)]
        copies.append(pltpu.make_async_copy(source, held_ref.at[pl.ds(first, last - first)], sem.at[1]))
    for copy in copies:
        copy.start()
    for copy in copies:
        copy.wait()


def fetch(w_gate, w_up, held, total, first, last, after):
    _, depth, width = w_gate.shape
    kept = [] if held is None else [in_vmem(held)]
    return pl.pallas_call(
        functools.partial(fetch_kernel, depth, first, last),
        out_shape=pltpu.VMEM((total, width), BF16),
        in_specs=[ANYWHERE] * 3 + [VMEM] * len(kept),
        out_specs=VMEM,
        scratch_shapes=[pltpu.SemaphoreType.DMA((2,))],
        input_output_aliases={3: 0} if kept else {},
        compiler_params=pltpu.CompilerParams(vmem_limit_bytes=VMEM_OWN),
        cost_estimate=pl.CostEstimate(flops=0, bytes_accessed=2 * (last - first) * width, transcendentals=0),
    )(w_gate, w_up, after, *kept)


def expert_kernel(
    n_local, chunk, own_ref, other_ref, held_ref, up_hbm, down_hbm, keep_ref, send_ref,
    ring, x_ref, acc_g, acc_u, act_ref, sem,
):
    half = own_ref.shape[0]
    _, depth, width = up_hbm.shape
    slots, parts = ring.shape[0], width // chunk
    have = held_ref.shape[0] - depth
    steps = [(True, at) for at in range(have, depth, chunk)] + [(False, at) for at in range(0, depth, chunk)]

    def copies(step):
        is_up, at = steps[step]
        slot = step % slots
        for p in range(parts):
            cut = pl.ds(p * chunk, chunk)
            source = up_hbm.at[0, pl.ds(at, chunk), cut] if is_up else down_hbm.at[0, cut, pl.ds(at, chunk)]
            yield pltpu.make_async_copy(source, ring.at[slot, cut], sem.at[slot, p])

    def start(step):
        for copy in copies(step):
            copy.start()

    for step in range(min(slots, len(steps))):
        start(step)
    x_ref[:half] = own_ref[:, :depth]
    x_ref[half:] = other_ref[:, :depth]
    shard_count = n_local // GROUP_EXPERTS
    mine = (lax.axis_index("node") * n_local + lax.axis_index("local")) // shard_count
    mine_hot = lax.broadcasted_iota(jnp.int32, (1, LANES), 1) == mine
    coeff = jnp.concatenate(
        [
            jnp.sum(jnp.where(mine_hot, ref[:, depth:].astype(F32), 0.0), axis=1, keepdims=True)
            for ref in (own_ref, other_ref)
        ],
        axis=0,
    )

    def add(acc, w_ref, row, column):
        rows, columns = w_ref.shape
        part = pl.ds(column, columns)
        product = jnp.dot(x_ref[:, row : row + rows], w_ref[...], preferred_element_type=F32)
        acc[:, part] = product if row == 0 else acc[:, part] + product

    for row in range(0, depth, chunk):
        add(acc_g, held_ref.at[pl.ds(row, chunk)], row, 0)
    for row in range(0, have, chunk):
        add(acc_u, held_ref.at[pl.ds(depth + row, chunk)], row, 0)
    for step, (is_up, at) in enumerate(steps):
        slot = step % slots
        for copy in copies(step):
            copy.wait()
        if is_up:
            for p in range(parts):
                add(acc_u, ring.at[slot, pl.ds(p * chunk, chunk)], at, p * chunk)
        else:
            if at == 0:
                gate_val = acc_g[...]
                act_ref[...] = (gate_val / (1.0 + jnp.exp(-gate_val)) * acc_u[...]).astype(BF16)
            piece = jnp.dot(act_ref[...], ring[slot], preferred_element_type=F32) * coeff
            keep_ref[:, pl.ds(at, chunk)] = piece[:half].astype(BF16)
            send_ref[:, pl.ds(at, chunk)] = piece[half:].astype(BF16)
        if step + slots < len(steps):
            start(step + slots)


def expert(own, other, held, w_up, w_down, chunk):
    half = own.shape[0]
    rows = 2 * half
    _, depth, width = w_up.shape
    slots = SLOTS
    return pl.pallas_call(
        functools.partial(expert_kernel, lax.axis_size("local"), chunk),
        out_shape=(jax.ShapeDtypeStruct((half, depth), BF16), jax.ShapeDtypeStruct((half, depth), BF16)),
        in_specs=[VMEM, VMEM, VMEM, ANYWHERE, ANYWHERE],
        out_specs=(VMEM, VMEM),
        scratch_shapes=[
            pltpu.VMEM((slots, width, chunk), BF16),
            pltpu.VMEM((rows, depth), BF16),
            pltpu.VMEM((rows, width), F32),
            pltpu.VMEM((rows, width), F32),
            pltpu.VMEM((rows, width), BF16),
            pltpu.SemaphoreType.DMA((slots, width // chunk)),
        ],
        compiler_params=pltpu.CompilerParams(vmem_limit_bytes=VMEM_OWN),
        cost_estimate=pl.CostEstimate(
            flops=6 * rows * depth * width, bytes_accessed=4 * depth * width, transcendentals=rows * width
        ),
    )(own, other, in_vmem(held), w_up, w_down)


def shards(attn_out, o_proj, resid, norm_gain, routes, route_w, w_gate, w_up, w_down):
    tok_rows, depth = resid.shape
    width = w_gate.shape[2]
    n_local = lax.axis_size("local")
    bits = [1 << b for b in range(n_local.bit_length() - 1)]
    w_gate, w_up, w_down = [pltpu.with_memory_space_constraint(w, pltpu.HBM) for w in (w_gate, w_up, w_down)]

    chunk = min(1024, width)
    total = depth + HAVE * chunk
    shares = [1] + [3] + [2] * (2 * len(bits) - 3) + [3, 1]
    unit = depth // 28
    cuts = [total // unit * sum(shares[:s]) // sum(shares) * unit for s in range(len(shares) + 1)]
    held, step = fetch(w_gate, w_up, None, total, 0, cuts[1], attn_out), 1
    attn_out, held = lax.optimization_barrier((attn_out, held))

    def send(x, axis, bit):
        nonlocal held, step
        got = swap(x, axis, bit)
        held = fetch(w_gate, w_up, held, total, cuts[step], cuts[step + 1], x)
        got, held = lax.optimization_barrier((got, held))
        step += 1
        return got

    keep, away, picks = project(attn_out, o_proj, routes, route_w)
    got = send(away, "local", bits[0])
    partial = keep + got.astype(F32)
    for bit in bits[1:-1]:
        half = partial.shape[0] // 2
        partial = partial[:half] + send(partial[half:].astype(BF16), "local", bit).astype(F32)
    partial = jnp.concatenate([partial[:tok_rows] + resid.astype(F32), partial[tok_rows:]], axis=0)
    out = jnp.concatenate(
        [partial, jnp.concatenate([picks, jnp.zeros((tok_rows, LANES), F32)], axis=0)], axis=1
    ).astype(BF16)
    got = send(out, "local", bits[-1]).astype(F32)
    got = jnp.concatenate([got[tok_rows:], got[:tok_rows]], axis=0)
    hidden = partial + got[:, :depth]
    columns = jnp.concatenate([picks, got[tok_rows:, depth:]], axis=0)
    mean_sq = jnp.mean(hidden * hidden, axis=-1, keepdims=True)
    normed = hidden * lax.rsqrt(mean_sq + 1e-06) * norm_gain
    tokens = jnp.concatenate([normed, columns], axis=1).astype(BF16)
    for bit in reversed(bits[:-1]):
        tokens = jnp.concatenate([tokens, send(tokens, "local", bit)], axis=0)
    other = send(tokens, "node", 1)

    keep, away = expert(tokens, other, held, w_up, w_down, chunk)
    keep = keep.astype(F32) + swap(away, "node", 1).astype(F32)
    for bit in bits:
        half = keep.shape[0] // 2
        keep = keep[:half] + swap(keep[half:].astype(BF16), "local", bit).astype(F32)
    return (hidden[:tok_rows] + keep).astype(BF16)


def solution(mesh):
    placed = (
        P(("rep", "node"), "local"),
        P("local", None),
        P(("rep", "node", "local"), None),
        P(),
        P(("rep", "node", "local"), None),
        P(("rep", "node", "local"), None),
        P(("node", "local"), None, None),
        P(("node", "local"), None, None),
        P(("node", "local"), None, None),
    )
    return jax.shard_map(
        shards,
        mesh=mesh,
        in_specs=placed,
        out_specs=P(("rep", "node", "local"), None),
        check_vma=False,
    )
```

```python
import functools

import jax
import jax.numpy as jnp
from jax import lax
from jax.experimental import pallas as pl
from jax.experimental.pallas import tpu as pltpu
from jax.sharding import PartitionSpec as P

GROUP_EXPERTS = 8
LANES = 128
VMEM_OWN = 26 << 20
SLOTS = 4
HAVE = 1
F32, BF16 = jnp.float32, jnp.bfloat16
VMEM = pl.BlockSpec(memory_space=pltpu.VMEM)
ANYWHERE = pl.BlockSpec(memory_space=pl.ANY)


def swap(x, axis, bit):
    return lax.ppermute(x, axis, [(i, i ^ bit) for i in range(lax.axis_size(axis))])


def in_vmem(x):
    return pltpu.with_memory_space_constraint(x, pltpu.VMEM)


def project_kernel(n_local, attn_ref, proj_ref, routes_ref, route_w_ref, keep_ref, send_ref, picks_ref):
    tok_rows, top = routes_ref.shape
    count = n_local * tok_rows
    here = lax.axis_index("local")
    place = lax.broadcasted_iota(jnp.int32, (count, count), 0)
    block, flip = place // tok_rows, 0
    bits = n_local.bit_length() - 1
    for b in range(bits):
        flip = flip | (((block >> b) & 1) << (bits - 1 - b))
    owner = (here ^ flip) * tok_rows + place % tok_rows
    order = (owner == lax.broadcasted_iota(jnp.int32, (count, count), 1)).astype(BF16)
    ordered = jnp.dot(order, attn_ref[...], preferred_element_type=F32).astype(BF16)
    half = count // 2
    partial = jnp.dot(ordered, proj_ref[...], preferred_element_type=F32)
    keep_ref[...] = partial[:half]
    send_ref[...] = partial[half:].astype(BF16)
    lane = lax.broadcasted_iota(jnp.int32, (tok_rows, LANES), 1)
    total = jnp.zeros((tok_rows, LANES), F32)
    weights = route_w_ref[...].astype(F32)
    for k in range(top):
        total = total + jnp.where(routes_ref[:, k : k + 1] == lane, weights[:, k : k + 1], 0.0)
    picks_ref[...] = total


def project(attn_out, o_proj, routes, route_w):
    depth = o_proj.shape[1]
    half = attn_out.shape[0] // 2
    return pl.pallas_call(
        functools.partial(project_kernel, lax.axis_size("local")),
        out_shape=(
            pltpu.VMEM((half, depth), F32),
            pltpu.VMEM((half, depth), BF16),
            pltpu.VMEM((routes.shape[0], LANES), F32),
        ),
        in_specs=[VMEM] * 4,
        out_specs=(VMEM, VMEM, VMEM),
        compiler_params=pltpu.CompilerParams(vmem_limit_bytes=VMEM_OWN),
    )(attn_out, o_proj, routes, route_w)


def fetch_kernel(depth, first, last, gate_hbm, up_hbm, after_ref, *refs):
    held_ref, sem = refs[-2:]
    copies = []
    if first < depth:
        part = pl.ds(first, min(last, depth) - first)
        copies.append(pltpu.make_async_copy(gate_hbm.at[0, part], held_ref.at[part], sem.at[0]))
    if last > depth:
        first = max(first, depth)
        source = up_hbm.at[0, pl.ds(first - depth, last - first)]
        copies.append(pltpu.make_async_copy(source, held_ref.at[pl.ds(first, last - first)], sem.at[1]))
    for copy in copies:
        copy.start()
    for copy in copies:
        copy.wait()


def fetch(w_gate, w_up, held, total, first, last, after):
    _, depth, width = w_gate.shape
    kept = [] if held is None else [in_vmem(held)]
    return pl.pallas_call(
        functools.partial(fetch_kernel, depth, first, last),
        out_shape=pltpu.VMEM((total, width), BF16),
        in_specs=[ANYWHERE] * 3 + [VMEM] * len(kept),
        out_specs=VMEM,
        scratch_shapes=[pltpu.SemaphoreType.DMA((2,))],
        input_output_aliases={3: 0} if kept else {},
        compiler_params=pltpu.CompilerParams(vmem_limit_bytes=VMEM_OWN),
        cost_estimate=pl.CostEstimate(flops=0, bytes_accessed=2 * (last - first) * width, transcendentals=0),
    )(w_gate, w_up, after, *kept)


def expert_kernel(
    n_local, chunk, own_ref, other_ref, held_ref, up_hbm, down_hbm, keep_ref, send_ref,
    ring, x_ref, acc_g, acc_u, act_ref, sem,
):
    half = own_ref.shape[0]
    _, depth, width = up_hbm.shape
    slots, parts = ring.shape[0], width // chunk
    have = held_ref.shape[0] - depth
    steps = [(True, at) for at in range(have, depth, chunk)] + [(False, at) for at in range(0, depth, chunk)]

    def copies(step):
        is_up, at = steps[step]
        slot = step % slots
        for p in range(parts):
            cut = pl.ds(p * chunk, chunk)
            source = up_hbm.at[0, pl.ds(at, chunk), cut] if is_up else down_hbm.at[0, cut, pl.ds(at, chunk)]
            yield pltpu.make_async_copy(source, ring.at[slot, cut], sem.at[slot, p])

    def start(step):
        for copy in copies(step):
            copy.start()

    for step in range(min(slots, len(steps))):
        start(step)
    x_ref[:half] = own_ref[:, :depth]
    x_ref[half:] = other_ref[:, :depth]
    shard_count = n_local // GROUP_EXPERTS
    mine = (lax.axis_index("node") * n_local + lax.axis_index("local")) // shard_count
    mine_hot = lax.broadcasted_iota(jnp.int32, (1, LANES), 1) == mine
    coeff = jnp.concatenate(
        [
            jnp.sum(jnp.where(mine_hot, ref[:, depth:].astype(F32), 0.0), axis=1, keepdims=True)
            for ref in (own_ref, other_ref)
        ],
        axis=0,
    )

    def add(acc, w_ref, row, column):
        rows, columns = w_ref.shape
        part = pl.ds(column, columns)
        product = jnp.dot(x_ref[:, row : row + rows], w_ref[...], preferred_element_type=F32)
        acc[:, part] = product if row == 0 else acc[:, part] + product

    for row in range(0, depth, chunk):
        add(acc_g, held_ref.at[pl.ds(row, chunk)], row, 0)
    for row in range(0, have, chunk):
        add(acc_u, held_ref.at[pl.ds(depth + row, chunk)], row, 0)
    for step, (is_up, at) in enumerate(steps):
        slot = step % slots
        for copy in copies(step):
            copy.wait()
        if is_up:
            for p in range(parts):
                add(acc_u, ring.at[slot, pl.ds(p * chunk, chunk)], at, p * chunk)
        else:
            if at == 0:
                gate_val = acc_g[...]
                act_ref[...] = (gate_val / (1.0 + jnp.exp(-gate_val)) * acc_u[...]).astype(BF16)
            piece = jnp.dot(act_ref[...], ring[slot], preferred_element_type=F32) * coeff
            keep_ref[:, pl.ds(at, chunk)] = piece[:half].astype(BF16)
            send_ref[:, pl.ds(at, chunk)] = piece[half:].astype(BF16)
        if step + slots < len(steps):
            start(step + slots)


def expert(own, other, held, w_up, w_down, chunk):
    half = own.shape[0]
    rows = 2 * half
    _, depth, width = w_up.shape
    slots = SLOTS
    return pl.pallas_call(
        functools.partial(expert_kernel, lax.axis_size("local"), chunk),
        out_shape=(jax.ShapeDtypeStruct((half, depth), BF16), pltpu.VMEM((half, depth), BF16)),
        in_specs=[VMEM, VMEM, VMEM, ANYWHERE, ANYWHERE],
        out_specs=(VMEM, VMEM),
        scratch_shapes=[
            pltpu.VMEM((slots, width, chunk), BF16),
            pltpu.VMEM((rows, depth), BF16),
            pltpu.VMEM((rows, width), F32),
            pltpu.VMEM((rows, width), F32),
            pltpu.VMEM((rows, width), BF16),
            pltpu.SemaphoreType.DMA((slots, width // chunk)),
        ],
        compiler_params=pltpu.CompilerParams(vmem_limit_bytes=VMEM_OWN),
        cost_estimate=pl.CostEstimate(
            flops=6 * rows * depth * width, bytes_accessed=4 * depth * width, transcendentals=rows * width
        ),
    )(own, other, in_vmem(held), w_up, w_down)


def shards(attn_out, o_proj, resid, norm_gain, routes, route_w, w_gate, w_up, w_down):
    tok_rows, depth = resid.shape
    width = w_gate.shape[2]
    n_local = lax.axis_size("local")
    bits = [1 << b for b in range(n_local.bit_length() - 1)]
    w_gate, w_up, w_down = [pltpu.with_memory_space_constraint(w, pltpu.HBM) for w in (w_gate, w_up, w_down)]

    chunk = min(1024, width)
    total = depth + HAVE * chunk
    shares = [1] + [3] + [2] * (2 * len(bits) - 3) + [3, 1]
    unit = depth // 28
    cuts = [total // unit * sum(shares[:s]) // sum(shares) * unit for s in range(len(shares) + 1)]
    held, step = fetch(w_gate, w_up, None, total, 0, cuts[1], attn_out), 1
    attn_out, held = lax.optimization_barrier((attn_out, held))

    def send(x, axis, bit):
        nonlocal held, step
        got = swap(x, axis, bit)
        held = fetch(w_gate, w_up, held, total, cuts[step], cuts[step + 1], x)
        got, held = lax.optimization_barrier((got, held))
        step += 1
        return got

    keep, away, picks = project(attn_out, o_proj, routes, route_w)
    got = send(away, "local", bits[0])
    partial = keep + got.astype(F32)
    for bit in bits[1:-1]:
        half = partial.shape[0] // 2
        partial = partial[:half] + send(partial[half:].astype(BF16), "local", bit).astype(F32)
    partial = jnp.concatenate([partial[:tok_rows] + resid.astype(F32), partial[tok_rows:]], axis=0)
    out = jnp.concatenate(
        [partial, jnp.concatenate([picks, jnp.zeros((tok_rows, LANES), F32)], axis=0)], axis=1
    ).astype(BF16)
    got = send(out, "local", bits[-1]).astype(F32)
    got = jnp.concatenate([got[tok_rows:], got[:tok_rows]], axis=0)
    hidden = partial + got[:, :depth]
    columns = jnp.concatenate([picks, got[tok_rows:, depth:]], axis=0)
    mean_sq = jnp.mean(hidden * hidden, axis=-1, keepdims=True)
    normed = hidden * lax.rsqrt(mean_sq + 1e-06) * norm_gain
    tokens = jnp.concatenate([normed, columns], axis=1).astype(BF16)
    for bit in reversed(bits[:-1]):
        tokens = jnp.concatenate([tokens, send(tokens, "local", bit)], axis=0)
    other = send(tokens, "node", 1)

    keep, away = expert(tokens, other, held, w_up, w_down, chunk)
    keep = keep.astype(F32) + swap(away, "node", 1).astype(F32)
    for bit in bits:
        half = keep.shape[0] // 2
        keep = keep[:half] + swap(keep[half:].astype(BF16), "local", bit).astype(F32)
    return (hidden[:tok_rows] + keep).astype(BF16)


def solution(mesh):
    placed = (
        P(("rep", "node"), "local"),
        P("local", None),
        P(("rep", "node", "local"), None),
        P(),
        P(("rep", "node", "local"), None),
        P(("rep", "node", "local"), None),
        P(("node", "local"), None, None),
        P(("node", "local"), None, None),
        P(("node", "local"), None, None),
    )
    return jax.shard_map(
        shards,
        mesh=mesh,
        in_specs=placed,
        out_specs=P(("rep", "node", "local"), None),
        check_vma=False,
    )
```
